32 devices in a mesh: grp: 2 (over x), req: 16 (over z, y, core).
Axes of the slice: x: 2, y: 2, z: 4, core: 2. Of those that a mesh axis runs over, the one named last changes fastest.
Arguments:
- moe_input: bfloat16 [512, 2048], P(('grp', 'req')), parts along dimension 0, may hold values from -6 to 6
- norm_gain: bfloat16 [2048], replicated, may hold values from 0.25 to 1.75
- route_ids: int32 [512, 8], P(('grp', 'req')), parts along dimension 0, may hold values from 0 to 15, all different within a row; in each aligned block of 16 rows (0 to 15, 16 to 31, ...) at most 16 rows name the same one
- route_gates: bfloat16 [512, 8], P(('grp', 'req')), parts along dimension 0, may hold values from 0.049804688 to 0.5
- expert_gate: bfloat16 [16, 2048, 768], P('req'), may hold values from -0.125 to 0.125
- expert_up: bfloat16 [16, 2048, 768], P('req'), may hold values from -0.125 to 0.125
- expert_down: bfloat16 [16, 768, 2048], P('req'), may hold values from -0.21875 to 0.21875
- queries: bfloat16 [128, 4096], P(('grp', 'req')), parts along dimension 0, may hold values from -4.5 to 4.5
- keys_cache: bfloat16 [128, 4, 384, 128], P(('grp', 'req')), parts along dimension 0, may hold values from -4.5 to 4.5
- values_cache: bfloat16 [128, 4, 384, 128], P(('grp', 'req')), parts along dimension 0, may hold values from -4.5 to 4.5
- new_keys: bfloat16 [128, 512], P(('grp', 'req')), parts along dimension 0, may hold values from -4.5 to 4.5
- new_values: bfloat16 [128, 512], P(('grp', 'req')), parts along dimension 0, may hold values from -4.5 to 4.5
- cache_lengths: int32 [128], P(('grp', 'req')), parts along dimension 0, may hold values from 1 to 384
Outputs:
- moe_out: bfloat16 [512, 2048], P(('grp', 'req')), parts along dimension 0
- attention_out: bfloat16 [128, 4096], P(('grp', 'req')), parts along dimension 0
The draws below stay inside these ranges and needn't reach their ends.
There are 2 independent parts, one for each index of `grp`. The reference program is written for one: setup_inputs(seed, part) draws one part's arguments, and reference() takes and returns one part's arrays. A program takes and returns all parts, laid end to end along the dimension named above; an argument that names none is the same for every part. Nothing has to cross between parts.
Inputs may be any that keep to these rules, and one draw needn't show every extreme that they name: `route_ids`: each row names 8 different experts; in each aligned block of 16 rows (the rows of one device) no expert is named by more than 16 rows, a bound that some block reaches.
All inputs are finite; a program needn't handle non-finite values.
Results may differ from the reference program's by a relative error of at most 0.0065.
Values may be sent and summed in bfloat16 or wider, within the bound.
A program may use at most 64 MiB of HBM per device.

```python
import math
import jax
import jax.numpy as jnp
import numpy as np
from jax import lax

D = 2048
FF = 768
QH = 32
KVH = 4
HD = 128
TOP = 8
L_MAX = 384
R_DEV = 16
EXPERTS = 16
CAP = 16
QPK = 8
ROWS = 256
ROWS_B = 64
N_REQ = 16


def attention_draw(key):
    query_key = jax.random.fold_in(key, 11)
    cache_key = jax.random.fold_in(key, 12)
    fresh_key = jax.random.fold_in(key, 13)
    queries = jax.random.truncated_normal(query_key, -4.5, 4.5, (ROWS_B, QH * HD), jnp.float32)
    cached = jax.random.truncated_normal(cache_key, -4.5, 4.5, (ROWS_B, KVH, L_MAX, HD), jnp.float32)
    fresh = jax.random.truncated_normal(fresh_key, -4.5, 4.5, (ROWS_B, KVH * HD), jnp.float32)
    return (queries, cached, fresh)


def draw_queries(key, part):
    return attention_draw(key)[0].astype(jnp.bfloat16)


def draw_keys_cache(key, part):
    return attention_draw(key)[1].astype(jnp.bfloat16)


def draw_new_keys(key, part):
    return attention_draw(key)[2].astype(jnp.bfloat16)


def plant(entries, own_key, least, top_value):
    longest = entries.shape.index(max(entries.shape))
    spots = []
    for shift in (0, 1):
        where = [jax.random.randint(jax.random.fold_in(own_key, axis), (), 0, length) for axis, length in enumerate(entries.shape)]
        where[longest] = (where[longest] + shift) % entries.shape[longest]
        spots.append(tuple(where))
    return entries.at[spots[0]].set(least).at[spots[1]].set(top_value)


def block_levels(own_key, shape, pieces, least, largest):
    gain = 1.0
    for axis_at, parts in pieces:
        draws = jax.random.uniform(jax.random.fold_in(jax.random.fold_in(own_key, 6), axis_at), (parts,), jnp.float32, least / len(pieces), largest / len(pieces))
        gain = gain * jnp.repeat(jnp.exp(draws), shape[axis_at] // parts).reshape((-1,) + (1,) * (len(shape) - 1 - axis_at))
    return gain


def deal_out(key, own, number, rows, amount, top, limit, lean):
    order = jax.random.permutation(key, amount)
    crowded, usual = load_shares(amount, rows * top, limit, lean, True), load_shares(amount, rows * top, limit, lean, False)
    places = jnp.arange(amount)

    def named(sizes, turn):
        used = int((sizes > 0).sum())
        fixed = max(1, used // 4)
        shifted = fixed + (places - fixed + turn * (used - fixed)) % max(1, amount - fixed)
        return jnp.zeros((amount,), jnp.int32).at[order[jnp.where(places < fixed, places, shifted)]].set(jnp.asarray(sizes, jnp.int32))

    sizes = jnp.where(number % 4 == 0, named(crowded, number // 4), named(usual, number - number // 4 - 1))
    mixed = jax.random.permutation(jax.random.fold_in(own, 3), amount)
    giver, sink = mixed[0:amount // 2 * 2:2], mixed[1:amount // 2 * 2:2]
    margin = jnp.minimum(sizes[giver] - 1, limit - sizes[sink]) // 2
    margin = jnp.where((giver == order[0]) | (sink == order[0]) | (sizes[sink] == 0), 0, jnp.maximum(margin, 0))
    shifted = jax.random.randint(jax.random.fold_in(own, 4), (amount // 2,), 0, 1 << 20) % (margin + 1)
    sizes = sizes.at[giver].add(-shifted).at[sink].add(shifted)
    members = jnp.searchsorted(jnp.cumsum(sizes), jnp.arange(rows * top), side="right").astype(jnp.int32)
    table = members.reshape(top, rows).T
    table = table[jax.random.permutation(jax.random.fold_in(own, 1), rows)]
    turn = jax.random.randint(jax.random.fold_in(own, 2), (rows, 1), 0, top)
    return jnp.take_along_axis(table, (jnp.arange(top)[None, :] + turn) % top, axis=1)


def load_shares(number_of, total, bound, slope, full):
    weights = [(1 << 20) // math.isqrt(rank ** slope) + 1 for rank in range(1, number_of + 1)]
    largest = bound if full else min(bound, max(-(-total // number_of), total * weights[0] // sum(weights)))
    least = 1 if total - largest >= number_of - 1 else 0
    given, surplus = [largest] + [least] * (number_of - 1), total - largest - least * (number_of - 1)
    while surplus > 0:
        movable = [i for i in range(1, number_of) if given[i] < largest] or [i for i in range(1, number_of) if given[i] < bound]
        whole, remaining = sum([weights[i] for i in movable]), surplus
        for i in movable:
            more = min(bound - given[i], max(1, remaining * weights[i] // whole), surplus)
            given[i] = given[i] + more
            surplus = surplus - more
    return np.array(given)


def bell_draw(own_key, extent, spread, reach, shards=(), held_as=jnp.bfloat16):
    values = jax.random.normal(own_key, extent, jnp.float32) * spread
    if len(shards) > 0:
        values = block_levels(own_key, extent, shards, -0.22, 0.18) * values
    return jnp.clip(values, min=-reach, max=reach).astype(held_as)


def setup_inputs(seed: int = 0, part: int = 0) -> dict:
    key_list = jax.random.split(jax.random.key(seed), 14)
    part_keys = jax.random.split(jax.random.fold_in(key_list[13], part), 14)
    moe_input = bell_draw(part_keys[0], (ROWS, D), 1.0, 6.0, ((0, 16),))
    norm_gain = jnp.clip(1.0 + 0.15 * jax.random.normal(key_list[1], (D,), jnp.float32), 0.25, 1.75).astype(jnp.bfloat16)
    route_ids_keys = jax.random.split(jax.random.fold_in(part_keys[2], 1), ROWS // R_DEV)
    route_ids_turns = jax.random.permutation(jax.random.fold_in(part_keys[2], 3), ROWS // R_DEV)
    route_ids = jax.vmap(lambda own, number: deal_out(jax.random.fold_in(part_keys[2], 2), own, number, R_DEV, EXPERTS, TOP, CAP, 2))(route_ids_keys, route_ids_turns).reshape((ROWS, TOP))
    route_gates = jnp.clip(0.049804688 + 0.4501953 * jax.random.uniform(part_keys[3], (ROWS, TOP), jnp.float32) ** block_levels(part_keys[3], (ROWS, TOP), ((0, 16),), -0.2, 0.2), 0.049804688, 0.5).astype(jnp.bfloat16)
    expert_gate = bell_draw(key_list[4], (EXPERTS, D, FF), D ** -0.5, 0.125, ((0, 16),))
    expert_up = bell_draw(key_list[5], (EXPERTS, D, FF), D ** -0.5, 0.125, ((0, 16),))
    expert_down = bell_draw(key_list[6], (EXPERTS, FF, D), FF ** -0.5, 0.21875, ((0, 16),))
    queries = draw_queries(jax.random.fold_in(jax.random.fold_in(key_list[13], part), 71), part)
    keys_cache = draw_keys_cache(jax.random.fold_in(jax.random.fold_in(key_list[13], part), 71), part)
    values_cache = bell_draw(part_keys[9], (ROWS_B, KVH, L_MAX, HD), 1.0, 4.5, ((0, 16),))
    new_keys = draw_new_keys(jax.random.fold_in(jax.random.fold_in(key_list[13], part), 71), part)
    new_values = bell_draw(part_keys[11], (ROWS_B, KVH * HD), 1.0, 4.5, ((0, 16),))
    cache_lengths = plant(jax.random.randint(part_keys[12], (ROWS_B,), 1, L_MAX + 1), jax.random.fold_in(part_keys[12], 1), 1, L_MAX).astype(jnp.int32)
    return dict(moe_input=moe_input, norm_gain=norm_gain, route_ids=route_ids, route_gates=route_gates, expert_gate=expert_gate, expert_up=expert_up, expert_down=expert_down, queries=queries, keys_cache=keys_cache, values_cache=values_cache, new_keys=new_keys, new_values=new_values, cache_lengths=cache_lengths)


EPS = 1e-06

def slot_table(route_ids, experts, capacity):
    onehot = (route_ids[:, :, None] == jnp.arange(experts, dtype=jnp.int32)[None, None, :]).astype(jnp.float32)
    present = lax.optimization_barrier(jnp.sum(onehot, axis=1))
    earlier = jnp.cumsum(present, axis=0) - present
    levels = jnp.arange(capacity, dtype=jnp.float32)
    placed = present[:, :, None] * (earlier[:, :, None] == levels[None, None, :]).astype(jnp.float32)
    return (onehot, placed)

def expert_rows(packed):
    w_gate, w_up, w_down, received = packed
    flat = received.reshape(-1, D)
    gate_part = jnp.dot(flat, w_gate, preferred_element_type=jnp.float32)
    up_part = jnp.dot(flat, w_up, preferred_element_type=jnp.float32)
    active = (jax.nn.silu(gate_part) * up_part).astype(jnp.bfloat16)
    produced = jnp.dot(active, w_down, preferred_element_type=jnp.float32).astype(jnp.bfloat16)
    return produced.reshape(received.shape)

def attend(queries, keys_cache, values_cache, new_keys, new_values, cache_lengths):
    batch_rows = queries.shape[0]
    score_scale = HD ** (-0.5)
    grouped = queries.astype(jnp.float32).reshape(batch_rows, KVH, QPK, HD)
    scores = jnp.einsum('bgqd,bgld->bgql', grouped, keys_cache.astype(jnp.float32)) * score_scale
    own_score = jnp.einsum('bgqd,bgd->bgq', grouped, new_keys.astype(jnp.float32).reshape(batch_rows, KVH, HD)) * score_scale
    live_mask = (jnp.arange(L_MAX, dtype=jnp.int32)[None, :] < cache_lengths[:, None])[:, None, None, :]
    highest = jnp.maximum(lax.optimization_barrier(jnp.max(jnp.where(live_mask, scores, -jnp.inf), axis=-1)), own_score)
    weights = jnp.where(live_mask, jnp.exp(scores - highest[..., None]), 0.0)
    own_weight = jnp.exp(own_score - highest)
    totals = lax.optimization_barrier(jnp.sum(weights, axis=-1)) + own_weight
    prob_low = (weights / totals[..., None]).astype(jnp.bfloat16)
    own_prob = (own_weight / totals).astype(jnp.bfloat16)
    mixed_out = jnp.einsum('bgql,bgld->bgqd', prob_low.astype(jnp.float32), values_cache.astype(jnp.float32))
    mixed_out = mixed_out + own_prob.astype(jnp.float32)[..., None] * new_values.astype(jnp.float32).reshape(batch_rows, KVH, 1, HD)
    return mixed_out.reshape(batch_rows, QH * HD).astype(jnp.bfloat16)

def reference(moe_input, norm_gain, route_ids, route_gates, expert_gate, expert_up, expert_down, queries, keys_cache, values_cache, new_keys, new_values, cache_lengths):
    hidden = moe_input.astype(jnp.float32)
    normed = (hidden * lax.rsqrt(lax.optimization_barrier(jnp.mean(hidden * hidden, axis=-1, keepdims=True)) + EPS) * norm_gain.astype(jnp.float32)).astype(jnp.bfloat16)
    blocks = normed.reshape(N_REQ, R_DEV, D)
    id_blocks = route_ids.reshape(N_REQ, R_DEV, TOP)
    onehot, placed = jax.vmap(lambda block_ids: slot_table(block_ids, EXPERTS, CAP))(id_blocks)
    sent = jnp.einsum('nrec,nrd->necd', placed, blocks.astype(jnp.float32)).astype(jnp.bfloat16)
    produced = lax.map(expert_rows, (expert_gate, expert_up, expert_down, jnp.swapaxes(sent, 0, 1)))
    returned = jnp.swapaxes(produced, 0, 1)
    gate_blocks = route_gates.astype(jnp.float32).reshape(N_REQ, R_DEV, TOP)
    weight = jnp.einsum('nrke,nrk->nre', onehot, gate_blocks)
    combine = weight[..., None] * placed
    expert_sum = jnp.einsum('nrec,necd->nrd', combine, returned.astype(jnp.float32))
    moe_out = (hidden + expert_sum.reshape(ROWS, D)).astype(jnp.bfloat16)
    attention_out = attend(queries, keys_cache, values_cache, new_keys, new_values, cache_lengths)
    return (moe_out, attention_out)
```

```python
import functools
import jax
import jax.numpy as jnp
from jax import lax
from jax.experimental import pallas as pl
from jax.experimental.pallas import tpu as pltpu
from jax.sharding import PartitionSpec as P

EPS = 1e-06
F32 = jnp.float32
BF16 = jnp.bfloat16


def push(src, dst, send, recv, peer):
    copy = pltpu.make_async_remote_copy(
        src_ref=src,
        dst_ref=dst,
        send_sem=send,
        recv_sem=recv,
        device_id={"req": peer},
        device_id_type=pl.DeviceIdType.MESH,
    )
    copy.start()
    return copy


def kernel(
    n,
    moe_ref,
    gain_ref,
    ids_ref,
    gates_ref,
    wg_hbm,
    wu_hbm,
    wd_hbm,
    q_ref,
    k_hbm,
    v_hbm,
    nk_ref,
    nv_ref,
    len_ref,
    out_ref,
    att_ref,
    wg,
    wu,
    wd,
    kc,
    vc,
    rows,
    part,
    rcore,
    ry,
    total,
    rz,
    load_sem,
    zs,
    zr,
    ys,
    yr,
    cs,
    cr,
    bzs,
    bzr,
    bys,
    byr,
    bcs,
    bcr,
):
    block, width = moe_ref.shape
    local = wg.shape[0]
    far = n // 4
    half = n // 2
    lanes = rows.shape[-1] - width
    me = lax.axis_index("req")
    c, y, f = lax.rem(me, 2), lax.rem(me // 2, 2), me // 4
    sibling = me + 1 - 2 * c
    across = me + 2 - 4 * y

    def place(step):
        return lax.rem(f + step, far)

    def away(step):
        return place(step) * 4 + y * 2 + c

    loads = [
        pltpu.make_async_copy(src, dst, load_sem.at[i])
        for i, (src, dst) in enumerate(
            ((k_hbm, kc), (v_hbm, vc), (wg_hbm, wg), (wu_hbm, wu), (wd_hbm, wd))
        )
    ]
    for load in loads:
        load.start()

    barrier = pltpu.get_barrier_semaphore()
    for peer in [away(s) for s in range(1, far)] + [across, sibling]:
        pl.semaphore_signal(
            barrier, inc=1, device_id={"req": peer}, device_id_type=pl.DeviceIdType.MESH
        )

    hidden = moe_ref[...].astype(F32)
    scale = lax.rsqrt(jnp.mean(hidden * hidden, axis=-1, keepdims=True) + EPS)
    mine = y * far + f
    rows[c, mine, :, 0:width] = (hidden * scale * gain_ref[...].astype(F32)).astype(BF16)
    ids = ids_ref[...]
    gates = gates_ref[...].astype(F32)
    column = lax.broadcasted_iota(jnp.int32, (block, lanes), 1)
    weight = jnp.zeros((block, lanes), F32)
    for k in range(ids.shape[1]):
        weight = weight + jnp.where(column == ids[:, k : k + 1], gates[:, k : k + 1], 0.0)
    rows[c, mine, :, width:] = weight.astype(BF16)
    pl.semaphore_wait(barrier, far + 1)

    own = rows.at[c, mine]
    to_z = [push(own, own, zs.at[s], zr.at[s], away(s)) for s in range(1, far)]
    to_y = [push(own, own, ys.at[0], yr.at[0], across)]

    batch, heads, span, size = kc.shape
    group = q_ref.shape[1] // (heads * size)
    tall = group * batch
    root = size ** (-0.5)
    row_batch = lax.rem(lax.broadcasted_iota(jnp.int32, (tall, span), 0), batch)
    position = lax.broadcasted_iota(jnp.int32, (tall, span), 1)
    live = [(row_batch == b) & (position < len_ref[b]) for b in range(batch)]

    def attend(g):
        q = q_ref[:, g * group * size : (g + 1) * group * size].astype(F32)
        q = jnp.concatenate([q[:, h * size : (h + 1) * size] for h in range(group)], axis=0)
        nk = nk_ref[:, g * size : (g + 1) * size].astype(F32)
        nv = nv_ref[:, g * size : (g + 1) * size].astype(F32)
        nk = jnp.concatenate([nk] * group, axis=0)
        nv = jnp.concatenate([nv] * group, axis=0)
        own_score = jnp.sum(q * nk, axis=-1, keepdims=True) * root
        q = q.astype(BF16)
        scores = [
            lax.dot_general(
                q, kc[b, g], (((1,), (1,)), ((), ())), preferred_element_type=F32
            )
            * root
            for b in range(batch)
        ]
        top = own_score
        for b in range(batch):
            masked = jnp.where(live[b], scores[b], -jnp.inf)
            top = jnp.maximum(top, jnp.max(masked, axis=-1, keepdims=True))
        weights = [jnp.where(live[b], jnp.exp(scores[b] - top), 0.0) for b in range(batch)]
        own_weight = jnp.exp(own_score - top)
        totals = own_weight
        for b in range(batch):
            totals = totals + jnp.sum(weights[b], axis=-1, keepdims=True)
        mixed = (own_weight / totals).astype(BF16).astype(F32) * nv
        for b in range(batch):
            mixed = mixed + jnp.dot(
                (weights[b] / totals).astype(BF16), vc[b, g], preferred_element_type=F32
            )
        flat = [mixed[h * batch : (h + 1) * batch, :] for h in range(group)]
        att_ref[:, g * group * size : (g + 1) * group * size] = jnp.concatenate(
            flat, axis=1
        ).astype(BF16)

    loads[0].wait()
    loads[1].wait()
    first, second = (heads + 1) // 2, heads
    attend(0)
    for s in range(1, far):
        to_z[s - 1].wait_recv()
        got = rows.at[c, y * far + place(far - s)]
        to_y.append(push(got, got, ys.at[s], yr.at[s], across))
    near = rows.at[c, pl.ds(y * far, far)]
    to_core = [push(near, near, cs.at[0], cr.at[0], sibling)]
    for g in range(1, first):
        attend(g)
    for s in range(far):
        to_y[s].wait_recv()
    near = rows.at[c, pl.ds((1 - y) * far, far)]
    to_core.append(push(near, near, cs.at[1], cr.at[1], sibling))
    for load in loads[2:]:
        load.wait()

    step = min(half, 8)
    tile = 512 if width % 512 == 0 else width

    def experts(side):
        def chunk(i, carry):
            at = pl.ds(i * step, step)
            x = rows[side, at, :, 0:width].reshape(step * block, width)
            table = rows[side, at, :, width:].reshape(step * block, lanes).astype(F32)
            number = lax.broadcasted_iota(jnp.int32, table.shape, 1)
            active, chosen = [], []
            for e in range(local):
                gate = jnp.dot(x, wg[e], preferred_element_type=F32)
                up = jnp.dot(x, wu[e], preferred_element_type=F32)
                active.append((gate / (1.0 + jnp.exp(-gate)) * up).astype(BF16))
                picked = jnp.where(number == me * local + e, table, 0.0)
                chosen.append(jnp.sum(picked, axis=-1, keepdims=True))
            for t in range(0, width, tile):
                got = jnp.zeros((step * block, tile), F32)
                for e in range(local):
                    made = jnp.dot(active[e], wd[e, :, t : t + tile], preferred_element_type=F32)
                    got = got + chosen[e] * made.astype(BF16).astype(F32)
                part[side, at, :, t : t + tile] = got.astype(BF16).reshape(step, block, tile)
            return carry

        lax.fori_loop(0, half // step, chunk, 0)

    experts(c)
    to_core[0].wait_recv()
    to_core[1].wait_recv()
    experts(1 - c)

    back_core = push(part.at[1 - c], rcore, bcs, bcr, sibling)
    for g in range(first, second):
        attend(g)
    back_core.wait_recv()

    back_y = []
    for s in [*range(1, far), 0]:
        at = (1 - y) * far + place(s)
        part[c, at] = (part[c, at].astype(F32) + rcore[at].astype(F32)).astype(BF16)
        back_y.append(push(part.at[c, at], ry.at[s], bys.at[s], byr.at[s], across))
    back_z = []
    for s, arrived in zip([*range(1, far), 0], back_y):
        at = y * far + place(s)
        kept = part[c, at].astype(F32) + rcore[at].astype(F32)
        arrived.wait_recv()
        kept = kept + ry[s].astype(F32)
        if s:
            total[s - 1] = kept.astype(BF16)
            back_z.append(push(total.at[s - 1], rz.at[s - 1], bzs.at[s], bzr.at[s], away(s)))
    result = moe_ref[...].astype(F32) + kept
    for s in range(1, far):
        back_z[s - 1].wait_recv()
        result = result + rz[s - 1].astype(F32)
    out_ref[...] = result.astype(BF16)
    for copy in [*to_z, *to_y, *to_core, back_core, *back_y, *back_z]:
        copy.wait_send()


def body(*args):
    moe, gain, ids, gates, wg, wu, wd, q, k, v, nk, nv, lengths = args
    n = lax.axis_size("req")
    block, width = moe.shape
    experts = n * wg.shape[0]
    lanes = -(-experts // 128) * 128
    far, half = n // 4, n // 2
    vmem = pl.BlockSpec(memory_space=pltpu.VMEM)
    hbm = pl.BlockSpec(memory_space=pl.ANY)
    smem = pl.BlockSpec(memory_space=pltpu.SMEM)
    many = pltpu.SemaphoreType.DMA((far,))
    return pl.pallas_call(
        functools.partial(kernel, n),
        out_shape=(
            jax.ShapeDtypeStruct(moe.shape, BF16),
            jax.ShapeDtypeStruct(q.shape, BF16),
        ),
        in_specs=[vmem, vmem, vmem, vmem, hbm, hbm, hbm, vmem, hbm, hbm, vmem, vmem, smem],
        out_specs=(vmem, vmem),
        scratch_shapes=[
            pltpu.VMEM(wg.shape, BF16),
            pltpu.VMEM(wu.shape, BF16),
            pltpu.VMEM(wd.shape, BF16),
            pltpu.VMEM(k.shape, BF16),
            pltpu.VMEM(v.shape, BF16),
            pltpu.VMEM((2, half, block, width + lanes), BF16),
            pltpu.VMEM((2, half, block, width), BF16),
            pltpu.VMEM((half, block, width), BF16),
            pltpu.VMEM((far, block, width), BF16),
            pltpu.VMEM((far - 1, block, width), BF16),
            pltpu.VMEM((far - 1, block, width), BF16),
            pltpu.SemaphoreType.DMA((5,)),
            many,
            many,
            many,
            many,
            pltpu.SemaphoreType.DMA((2,)),
            pltpu.SemaphoreType.DMA((2,)),
            many,
            many,
            many,
            many,
            pltpu.SemaphoreType.DMA,
            pltpu.SemaphoreType.DMA,
        ],
        compiler_params=pltpu.CompilerParams(
            collective_id=0, has_side_effects=True, vmem_limit_bytes=58 * 1024 * 1024
        ),
    )(moe, gain.reshape(1, width), ids, gates, wg, wu, wd, q, k, v, nk, nv, lengths)


def solution(mesh):
    in_specs = (
        P(("grp", "req"), None),
        P(),
        P(("grp", "req"), None),
        P(("grp", "req"), None),
        P("req", None, None),
        P("req", None, None),
        P("req", None, None),
        P(("grp", "req"), None),
        P(("grp", "req"), None, None, None),
        P(("grp", "req"), None, None, None),
        P(("grp", "req"), None),
        P(("grp", "req"), None),
        P(("grp", "req")),
    )
    out_specs = (P(("grp", "req"), None), P(("grp", "req"), None))
    return jax.shard_map(body, mesh=mesh, in_specs=in_specs, out_specs=out_specs, check_vma=False)
```

```python
import functools
import jax
import jax.numpy as jnp
from jax import lax
from jax.experimental import pallas as pl
from jax.experimental.pallas import tpu as pltpu
from jax.sharding import PartitionSpec as P

EPS = 1e-06
F32 = jnp.float32
BF16 = jnp.bfloat16


def link(src, dst, send, recv, peer):
    return pltpu.make_async_remote_copy(
        src_ref=src,
        dst_ref=dst,
        send_sem=send,
        recv_sem=recv,
        device_id={"req": peer},
        device_id_type=pl.DeviceIdType.MESH,
    )


def push(*args):
    copy = link(*args)
    copy.start()
    return copy


def flip(index, bit):
    return index + bit - 2 * bit * lax.rem(index // bit, 2)


def low_bit(offset):
    return offset & -offset


def spread(a_ref, b_ref, a_out, b_out, sem):
    copies = [
        pltpu.make_async_copy(a_ref, a_out, sem.at[0]),
        pltpu.make_async_copy(b_ref, b_out, sem.at[1]),
    ]
    for copy in copies:
        copy.start()
    for copy in copies:
        copy.wait()


def kernel(
    n,
    moe_ref,
    gain_ref,
    ids_ref,
    gates_ref,
    wg_hbm,
    wu_hbm,
    wd_hbm,
    q_ref,
    k_hbm,
    v_hbm,
    nk_ref,
    nv_ref,
    len_ref,
    out_ref,
    att_ref,
    wg,
    wu,
    wd,
    kc,
    vc,
    rows,
    part,
    rcore,
    ry,
    total,
    rz,
    load_sem,
    zs,
    zr,
    ys,
    yr,
    cs,
    cr,
    bzs,
    bzr,
    bys,
    byr,
    bcs,
    bcr,
):
    block, width = moe_ref.shape
    local = wg.shape[0]
    far = n // 4
    half = n // 2
    lanes = rows.shape[-1] - width
    me = lax.axis_index("req")
    c, y, f = lax.rem(me, 2), lax.rem(me // 2, 2), me // 4
    sibling = me + 1 - 2 * c
    across = me + 2 - 4 * y

    bits = [far >> (i + 1) for i in range(far.bit_length() - 1)]

    def below(offset):
        return [b for b in bits if not offset or b < low_bit(offset)]

    def place(offset):
        at = f
        for b in bits:
            if offset & b:
                at = flip(at, b)
        return at

    def hop(bit):
        return flip(f, bit) * 4 + y * 2 + c

    loads = [
        pltpu.make_async_copy(src, dst, load_sem.at[i])
        for i, (src, dst) in enumerate(
            ((k_hbm, kc), (v_hbm, vc), (wg_hbm, wg), (wu_hbm, wu), (wd_hbm, wd))
        )
    ]
    for load in loads:
        load.start()

    barrier = pltpu.get_barrier_semaphore()
    for peer in [hop(b) for b in bits] + [across, sibling]:
        pl.semaphore_signal(
            barrier, inc=1, device_id={"req": peer}, device_id_type=pl.DeviceIdType.MESH
        )

    hidden = moe_ref[...].astype(F32)
    scale = lax.rsqrt(jnp.mean(hidden * hidden, axis=-1, keepdims=True) + EPS)
    mine = y * far + f
    rows[c, mine, :, 0:width] = (hidden * scale * gain_ref[...].astype(F32).reshape(1, width)).astype(BF16)
    ids = ids_ref[...]
    gates = gates_ref[...].astype(F32)
    expert = lax.broadcasted_iota(jnp.int32, (lanes, block), 0)
    weight = jnp.zeros((lanes, block), F32)
    for k in range(ids.shape[0]):
        weight = weight + jnp.where(expert == ids[k : k + 1, :], gates[k : k + 1, :], 0.0)
    same = lax.broadcasted_iota(jnp.int32, (block, block), 0) == lax.broadcasted_iota(
        jnp.int32, (block, block), 1
    )
    rows[c, mine, :, width:] = lax.dot_general(
        same.astype(F32).astype(BF16),
        weight.astype(BF16),
        (((1,), (1,)), ((), ())),
        preferred_element_type=F32,
    ).astype(BF16)
    pl.semaphore_wait(barrier, len(bits) + 2)

    to_z, to_y, to_core = {}, {}, {}

    def relay(offset):
        got = rows.at[c, y * far + place(offset)]
        for b in below(offset):
            d = offset + b
            to_z[d] = push(got, got, zs.at[d], zr.at[d], hop(b))
        to_y[offset] = push(got, got, ys.at[offset], yr.at[offset], across)
        to_core[offset] = push(got, got, cs.at[offset], cr.at[offset], sibling)

    relay(0)

    batch, heads, span, size = kc.shape
    group = q_ref.shape[1] // (heads * size)
    tall = group * batch
    root = size ** (-0.5)
    row_batch = lax.rem(lax.broadcasted_iota(jnp.int32, (tall, span), 0), batch)
    position = lax.broadcasted_iota(jnp.int32, (tall, span), 1)
    live = [(row_batch == b) & (position < len_ref[b]) for b in range(batch)]

    def attend(g):
        q = q_ref[:, g * group * size : (g + 1) * group * size].astype(F32)
        q = jnp.concatenate([q[:, h * size : (h + 1) * size] for h in range(group)], axis=0)
        nk = nk_ref[:, g * size : (g + 1) * size].astype(F32)
        nv = nv_ref[:, g * size : (g + 1) * size].astype(F32)
        nk = jnp.concatenate([nk] * group, axis=0)
        nv = jnp.concatenate([nv] * group, axis=0)
        own_score = jnp.sum(q * nk, axis=-1, keepdims=True) * root
        q = q.astype(BF16)
        scores = [
            lax.dot_general(
                q, kc[b, g], (((1,), (1,)), ((), ())), preferred_element_type=F32
            )
            * root
            for b in range(batch)
        ]
        top = own_score
        for b in range(batch):
            masked = jnp.where(live[b], scores[b], -jnp.inf)
            top = jnp.maximum(top, jnp.max(masked, axis=-1, keepdims=True))
        weights = [jnp.where(live[b], jnp.exp(scores[b] - top), 0.0) for b in range(batch)]
        own_weight = jnp.exp(own_score - top)
        totals = own_weight
        for b in range(batch):
            totals = totals + jnp.sum(weights[b], axis=-1, keepdims=True)
        mixed = (own_weight / totals).astype(BF16).astype(F32) * nv
        for b in range(batch):
            mixed = mixed + jnp.dot(
                (weights[b] / totals).astype(BF16), vc[b, g], preferred_element_type=F32
            )
        flat = [mixed[h * batch : (h + 1) * batch, :] for h in range(group)]
        att_ref[:, g * group * size : (g + 1) * group * size] = jnp.concatenate(
            flat, axis=1
        ).astype(BF16)

    loads[0].wait()
    loads[1].wait()
    first, second = (heads + 1) // 2, heads
    attend(0)
    arrivals = sorted(range(1, far), key=lambda d: (-low_bit(d), d))
    for d in arrivals:
        to_z[d].wait_recv()
        relay(d)
    for g in range(1, first):
        attend(g)
    for d in [0, *arrivals]:
        to_y[d].wait_recv()
        got = rows.at[c, (1 - y) * far + place(d)]
        to_core[far + d] = push(got, got, cs.at[far + d], cr.at[far + d], sibling)
    for load in loads[2:]:
        load.wait()

    step = min(half, 8)
    tile = 512 if width % 512 == 0 else width

    def core_back(i, t):
        at = pl.ds(i * step, step)
        cut = pl.ds(t * tile, tile)
        return link(
            part.at[1 - c, at, :, cut],
            rcore.at[at, :, cut],
            bcs.at[i, t],
            bcr.at[i, t],
            sibling,
        )

    def experts(side, send):
        def chunk(i, carry):
            at = pl.ds(i * step, step)
            x = rows[side, at, :, 0:width].reshape(step * block, width)
            table = rows[side, at, :, width:].reshape(step * block, lanes).astype(F32)
            number = lax.broadcasted_iota(jnp.int32, table.shape, 1)
            active, chosen = [], []
            for e in range(local):
                gate = jnp.dot(x, wg[e], preferred_element_type=F32)
                up = jnp.dot(x, wu[e], preferred_element_type=F32)
                active.append((gate / (1.0 + jnp.exp(-gate)) * up).astype(BF16))
                picked = jnp.where(number == me * local + e, table, 0.0)
                chosen.append(jnp.sum(picked, axis=-1, keepdims=True))
            for t in range(0, width, tile):
                got = jnp.zeros((step * block, tile), F32)
                for e in range(local):
                    made = jnp.dot(active[e], wd[e, :, t : t + tile], preferred_element_type=F32)
                    got = got + chosen[e] * made.astype(BF16).astype(F32)
                part[side, at, :, t : t + tile] = got.astype(BF16).reshape(step, block, tile)
                if send:
                    core_back(i, t // tile).start()
            return carry

        lax.fori_loop(0, half // step, chunk, 0)

    experts(c, False)
    for copy in to_core.values():
        copy.wait_recv()
    experts(1 - c, True)

    for g in range(first, second):
        attend(g)
    back_core = [core_back(i, t) for i in range(half // step) for t in range(width // tile)]
    for copy in back_core:
        copy.wait_recv()

    back_y, back_z = {}, {}
    for d in reversed(range(far)):
        at = (1 - y) * far + place(d)
        part[c, at] = (part[c, at].astype(F32) + rcore[at].astype(F32)).astype(BF16)
        back_y[d] = push(part.at[c, at], ry.at[d], bys.at[d], byr.at[d], across)
    for d in reversed(range(far)):
        at = y * far + place(d)
        kept = part[c, at].astype(F32) + rcore[at].astype(F32)
        back_y[d].wait_recv()
        kept = kept + ry[d].astype(F32)
        for b in below(d):
            back_z[d + b].wait_recv()
            kept = kept + rz[d + b - 1].astype(F32)
        if d:
            total[d - 1] = kept.astype(BF16)
            back_z[d] = push(
                total.at[d - 1], rz.at[d - 1], bzs.at[d], bzr.at[d], hop(low_bit(d))
            )
    out_ref[...] = (moe_ref[...].astype(F32) + kept).astype(BF16)
    for copies in (to_z, to_y, to_core, back_y, back_z):
        for copy in copies.values():
            copy.wait_send()
    for copy in back_core:
        copy.wait_send()


def body(*args):
    moe, gain, ids, gates, wg, wu, wd, q, k, v, nk, nv, lengths = args
    n = lax.axis_size("req")
    block, width = moe.shape
    experts = n * wg.shape[0]
    lanes = -(-experts // 128) * 128
    far, half = n // 4, n // 2
    vmem = pl.BlockSpec(memory_space=pltpu.VMEM)
    hbm = pl.BlockSpec(memory_space=pl.ANY)
    smem = pl.BlockSpec(memory_space=pltpu.SMEM)
    many = pltpu.SemaphoreType.DMA((far,))
    step = min(half, 8)
    tile = 512 if width % 512 == 0 else width
    pieces = pltpu.SemaphoreType.DMA((half // step, width // tile))
    made = pl.pallas_call(
        functools.partial(kernel, n),
        out_shape=(
            jax.ShapeDtypeStruct(moe.shape, BF16),
            jax.ShapeDtypeStruct(q.shape, BF16),
        ),
        in_specs=[vmem, vmem, vmem, vmem, hbm, hbm, hbm, vmem, hbm, hbm, vmem, vmem, smem],
        out_specs=(vmem, vmem),
        scratch_shapes=[
            pltpu.VMEM(wg.shape, BF16),
            pltpu.VMEM(wu.shape, BF16),
            pltpu.VMEM(wd.shape, BF16),
            pltpu.VMEM(k.shape, BF16),
            pltpu.VMEM(v.shape, BF16),
            pltpu.VMEM((2, half, block, width + lanes), BF16),
            pltpu.VMEM((2, half, block, width), BF16),
            pltpu.VMEM((half, block, width), BF16),
            pltpu.VMEM((far, block, width), BF16),
            pltpu.VMEM((far - 1, block, width), BF16),
            pltpu.VMEM((far - 1, block, width), BF16),
            pltpu.SemaphoreType.DMA((5,)),
            many,
            many,
            many,
            many,
            pltpu.SemaphoreType.DMA((half,)),
            pltpu.SemaphoreType.DMA((half,)),
            many,
            many,
            many,
            many,
            pieces,
            pieces,
        ],
        compiler_params=pltpu.CompilerParams(
            collective_id=0, has_side_effects=True, vmem_limit_bytes=58 * 1024 * 1024
        ),
    )(moe, gain, ids.T, gates.T, wg, wu, wd, q, k, v, nk, nv, lengths)
    return pl.pallas_call(
        spread,
        out_shape=tuple(jax.ShapeDtypeStruct(a.shape, a.dtype) for a in made),
        in_specs=[hbm, hbm],
        out_specs=(hbm, hbm),
        scratch_shapes=[pltpu.SemaphoreType.DMA((2,))],
    )(*made)


def solution(mesh):
    in_specs = (
        P(("grp", "req"), None),
        P(),
        P(("grp", "req"), None),
        P(("grp", "req"), None),
        P("req", None, None),
        P("req", None, None),
        P("req", None, None),
        P(("grp", "req"), None),
        P(("grp", "req"), None, None, None),
        P(("grp", "req"), None, None, None),
        P(("grp", "req"), None),
        P(("grp", "req"), None),
        P(("grp", "req")),
    )
    out_specs = (P(("grp", "req"), None), P(("grp", "req"), None))
    return jax.shard_map(body, mesh=mesh, in_specs=in_specs, out_specs=out_specs, check_vma=False)
```

```python
import functools
import jax
import jax.numpy as jnp
from jax import lax
from jax.experimental import pallas as pl
from jax.experimental.pallas import tpu as pltpu
from jax.sharding import PartitionSpec as P

EPS = 1e-06
F32 = jnp.float32
BF16 = jnp.bfloat16


def link(src, dst, send, recv, peer):
    return pltpu.make_async_remote_copy(
        src_ref=src,
        dst_ref=dst,
        send_sem=send,
        recv_sem=recv,
        device_id={"req": peer},
        device_id_type=pl.DeviceIdType.MESH,
    )


def push(*args):
    copy = link(*args)
    copy.start()
    return copy


def flip(index, bit):
    return index + bit - 2 * bit * lax.rem(index // bit, 2)


def kernel(
    n,
    moe_hbm,
    gain_hbm,
    ids_hbm,
    gates_hbm,
    wg_hbm,
    wu_hbm,
    wd_hbm,
    q_hbm,
    k_hbm,
    v_hbm,
    nk_hbm,
    nv_hbm,
    len_hbm,
    out_hbm,
    att_hbm,
    moe_ref,
    gain_ref,
    ids_ref,
    gates_ref,
    q_ref,
    nk_ref,
    nv_ref,
    len_ref,
    out_ref,
    att_ref,
    wg,
    wu,
    wd,
    kc,
    vc,
    rows,
    part,
    rcore,
    ry,
    total,
    rz,
    small_sem,
    load_sem,
    zs,
    zr,
    ys,
    yr,
    cs,
    cr,
    bzs,
    bzr,
    bys,
    byr,
    bcs,
    bcr,
):
    block, width = moe_ref.shape
    local = wg.shape[0]
    far = n // 4
    half = n // 2
    lanes = rows.shape[-1] - width
    me = lax.axis_index("req")
    c, y, f = lax.rem(me, 2), lax.rem(me // 2, 2), me // 4
    sibling = me + 1 - 2 * c
    across = me + 2 - 4 * y

    bits = [far >> (i + 1) for i in range(far.bit_length() - 1)]

    def place(offset):
        at = f
        for b in bits:
            if offset & b:
                at = flip(at, b)
        return at

    def away(offset):
        return place(offset) * 4 + y * 2 + c

    small = [
        pltpu.make_async_copy(src, dst, small_sem.at[i])
        for i, (src, dst) in enumerate(
            (
                (moe_hbm, moe_ref),
                (gain_hbm, gain_ref),
                (ids_hbm, ids_ref),
                (gates_hbm, gates_ref),
                (q_hbm, q_ref),
                (nk_hbm, nk_ref),
                (nv_hbm, nv_ref),
                (len_hbm, len_ref),
            )
        )
    ]
    for load in small:
        load.start()
    barrier = pltpu.get_barrier_semaphore()
    for peer in [away(d) for d in range(1, far)] + [across, sibling]:
        pl.semaphore_signal(
            barrier, inc=1, device_id={"req": peer}, device_id_type=pl.DeviceIdType.MESH
        )

    loads = [
        pltpu.make_async_copy(src, dst, load_sem.at[i])
        for i, (src, dst) in enumerate(
            ((k_hbm, kc), (v_hbm, vc), (wg_hbm, wg), (wu_hbm, wu), (wd_hbm, wd))
        )
    ]
    for load in loads:
        load.start()

    for load in small[:4]:
        load.wait()
    hidden = moe_ref[...].astype(F32)
    scale = lax.rsqrt(jnp.mean(hidden * hidden, axis=-1, keepdims=True) + EPS)
    mine = y * far + f
    rows[c, mine, :, 0:width] = (hidden * scale * gain_ref[...].astype(F32).reshape(1, width)).astype(BF16)
    ids = ids_ref[...]
    gates = gates_ref[...].astype(F32)
    expert = lax.broadcasted_iota(jnp.int32, (lanes, block), 0)
    weight = jnp.zeros((lanes, block), F32)
    for k in range(ids.shape[0]):
        weight = weight + jnp.where(expert == ids[k : k + 1, :], gates[k : k + 1, :], 0.0)
    same = lax.broadcasted_iota(jnp.int32, (block, block), 0) == lax.broadcasted_iota(
        jnp.int32, (block, block), 1
    )
    rows[c, mine, :, width:] = lax.dot_general(
        same.astype(F32).astype(BF16),
        weight.astype(BF16),
        (((1,), (1,)), ((), ())),
        preferred_element_type=F32,
    ).astype(BF16)
    pl.semaphore_wait(barrier, far + 1)

    to_z, to_y, to_core = {}, {}, {}

    def relay(offset):
        got = rows.at[c, y * far + place(offset)]
        for d in range(1, far) if offset == 0 else ():
            to_z[d] = push(got, got, zs.at[d], zr.at[d], away(d))
        to_y[offset] = push(got, got, ys.at[offset], yr.at[offset], across)
        to_core[offset] = push(got, got, cs.at[offset], cr.at[offset], sibling)

    relay(0)
    for load in small[4:]:
        load.wait()

    batch, heads, span, size = kc.shape
    group = q_ref.shape[1] // (heads * size)
    tall = group * batch
    root = size ** (-0.5)
    row_batch = lax.rem(lax.broadcasted_iota(jnp.int32, (tall, span), 0), batch)
    position = lax.broadcasted_iota(jnp.int32, (tall, span), 1)
    live = [(row_batch == b) & (position < len_ref[b]) for b in range(batch)]

    def attend(g):
        q = q_ref[:, g * group * size : (g + 1) * group * size].astype(F32)
        q = jnp.concatenate([q[:, h * size : (h + 1) * size] for h in range(group)], axis=0)
        nk = nk_ref[:, g * size : (g + 1) * size].astype(F32)
        nv = nv_ref[:, g * size : (g + 1) * size].astype(F32)
        nk = jnp.concatenate([nk] * group, axis=0)
        nv = jnp.concatenate([nv] * group, axis=0)
        own_score = jnp.sum(q * nk, axis=-1, keepdims=True) * root
        q = q.astype(BF16)
        scores = [
            lax.dot_general(
                q, kc[b, g], (((1,), (1,)), ((), ())), preferred_element_type=F32
            )
            * root
            for b in range(batch)
        ]
        top = own_score
        for b in range(batch):
            masked = jnp.where(live[b], scores[b], -jnp.inf)
            top = jnp.maximum(top, jnp.max(masked, axis=-1, keepdims=True))
        weights = [jnp.where(live[b], jnp.exp(scores[b] - top), 0.0) for b in range(batch)]
        own_weight = jnp.exp(own_score - top)
        totals = own_weight
        for b in range(batch):
            totals = totals + jnp.sum(weights[b], axis=-1, keepdims=True)
        mixed = (own_weight / totals).astype(BF16).astype(F32) * nv
        for b in range(batch):
            mixed = mixed + jnp.dot(
                (weights[b] / totals).astype(BF16), vc[b, g], preferred_element_type=F32
            )
        flat = [mixed[h * batch : (h + 1) * batch, :] for h in range(group)]
        att_ref[:, g * group * size : (g + 1) * group * size] = jnp.concatenate(
            flat, axis=1
        ).astype(BF16)

    loads[0].wait()
    loads[1].wait()
    first, second = (heads + 1) // 2, heads
    attend(0)
    arrivals = range(1, far)
    for d in arrivals:
        to_z[d].wait_recv()
        relay(d)
    for g in range(1, first):
        attend(g)
    for d in [0, *arrivals]:
        to_y[d].wait_recv()
        got = rows.at[c, (1 - y) * far + place(d)]
        to_core[far + d] = push(got, got, cs.at[far + d], cr.at[far + d], sibling)
    for load in loads[2:]:
        load.wait()

    step = min(half, 8)
    tile = 512 if width % 512 == 0 else width

    def core_back(i, t):
        at = pl.ds(i * step, step)
        cut = pl.ds(t * tile, tile)
        return link(
            part.at[1 - c, at, :, cut],
            rcore.at[at, :, cut],
            bcs.at[i, t],
            bcr.at[i, t],
            sibling,
        )

    def experts(side, send):
        def chunk(i, carry):
            at = pl.ds(i * step, step)
            x = rows[side, at, :, 0:width].reshape(step * block, width)
            table = rows[side, at, :, width:].reshape(step * block, lanes).astype(F32)
            number = lax.broadcasted_iota(jnp.int32, table.shape, 1)
            active, chosen = [], []
            for e in range(local):
                gate = jnp.dot(x, wg[e], preferred_element_type=F32)
                up = jnp.dot(x, wu[e], preferred_element_type=F32)
                active.append((gate / (1.0 + jnp.exp(-gate)) * up).astype(BF16))
                picked = jnp.where(number == me * local + e, table, 0.0)
                chosen.append(jnp.sum(picked, axis=-1, keepdims=True))
            for t in range(0, width, tile):
                got = jnp.zeros((step * block, tile), F32)
                for e in range(local):
                    made = jnp.dot(active[e], wd[e, :, t : t + tile], preferred_element_type=F32)
                    got = got + chosen[e] * made.astype(BF16).astype(F32)
                part[side, at, :, t : t + tile] = got.astype(BF16).reshape(step, block, tile)
                if send:
                    core_back(i, t // tile).start()
            return carry

        lax.fori_loop(0, half // step, chunk, 0)

    experts(c, False)
    for copy in to_core.values():
        copy.wait_recv()
    experts(1 - c, True)

    for g in range(first, second):
        attend(g)
    att_copy = pltpu.make_async_copy(att_ref, att_hbm, small_sem.at[4])
    att_copy.start()
    back_core = [core_back(i, t) for i in range(half // step) for t in range(width // tile)]
    for copy in back_core:
        copy.wait_recv()

    back_y, back_z = {}, {}
    for d in reversed(range(far)):
        at = (1 - y) * far + place(d)
        part[c, at] = (part[c, at].astype(F32) + rcore[at].astype(F32)).astype(BF16)
        back_y[d] = push(part.at[c, at], ry.at[d], bys.at[d], byr.at[d], across)
    for d in reversed(range(far)):
        at = y * far + place(d)
        kept = part[c, at].astype(F32) + rcore[at].astype(F32)
        back_y[d].wait_recv()
        kept = kept + ry[d].astype(F32)
        if d:
            total[d - 1] = kept.astype(BF16)
            back_z[d] = push(total.at[d - 1], rz.at[d - 1], bzs.at[d], bzr.at[d], away(d))
    kept = moe_ref[...].astype(F32) + kept
    for d in range(1, far):
        back_z[d].wait_recv()
        kept = kept + rz[d - 1].astype(F32)
    out_ref[...] = kept.astype(BF16)
    out_copy = pltpu.make_async_copy(out_ref, out_hbm, small_sem.at[0])
    out_copy.start()
    for copies in (to_z, to_y, to_core, back_y, back_z):
        for copy in copies.values():
            copy.wait_send()
    for copy in back_core:
        copy.wait_send()
    att_copy.wait()
    out_copy.wait()


def body(*args):
    moe, gain, ids, gates, wg, wu, wd, q, k, v, nk, nv, lengths = args
    n = lax.axis_size("req")
    block, width = moe.shape
    experts = n * wg.shape[0]
    lanes = -(-experts // 128) * 128
    far, half = n // 4, n // 2
    hbm = pl.BlockSpec(memory_space=pl.ANY)
    many = pltpu.SemaphoreType.DMA((far,))
    step = min(half, 8)
    tile = 512 if width % 512 == 0 else width
    pieces = pltpu.SemaphoreType.DMA((half // step, width // tile))
    small = (moe, gain, ids.T, gates.T, q, nk, nv)
    return pl.pallas_call(
        functools.partial(kernel, n),
        out_shape=(
            jax.ShapeDtypeStruct(moe.shape, BF16),
            jax.ShapeDtypeStruct(q.shape, BF16),
        ),
        in_specs=[hbm] * 13,
        out_specs=(hbm, hbm),
        scratch_shapes=[
            *(pltpu.VMEM(a.shape, a.dtype) for a in small),
            pltpu.SMEM(lengths.shape, lengths.dtype),
            pltpu.VMEM(moe.shape, BF16),
            pltpu.VMEM(q.shape, BF16),
            pltpu.VMEM(wg.shape, BF16),
            pltpu.VMEM(wu.shape, BF16),
            pltpu.VMEM(wd.shape, BF16),
            pltpu.VMEM(k.shape, BF16),
            pltpu.VMEM(v.shape, BF16),
            pltpu.VMEM((2, half, block, width + lanes), BF16),
            pltpu.VMEM((2, half, block, width), BF16),
            pltpu.VMEM((half, block, width), BF16),
            pltpu.VMEM((far, block, width), BF16),
            pltpu.VMEM((far - 1, block, width), BF16),
            pltpu.VMEM((far - 1, block, width), BF16),
            pltpu.SemaphoreType.DMA((8,)),
            pltpu.SemaphoreType.DMA((5,)),
            many,
            many,
            many,
            many,
            pltpu.SemaphoreType.DMA((half,)),
            pltpu.SemaphoreType.DMA((half,)),
            many,
            many,
            many,
            many,
            pieces,
            pieces,
        ],
        compiler_params=pltpu.CompilerParams(
            collective_id=0, has_side_effects=True, vmem_limit_bytes=58 * 1024 * 1024
        ),
    )(moe, gain, ids.T, gates.T, wg, wu, wd, q, k, v, nk, nv, lengths)

def solution(mesh):
    in_specs = (
        P(("grp", "req"), None),
        P(),
        P(("grp", "req"), None),
        P(("grp", "req"), None),
        P("req", None, None),
        P("req", None, None),
        P("req", None, None),
        P(("grp", "req"), None),
        P(("grp", "req"), None, None, None),
        P(("grp", "req"), None, None, None),
        P(("grp", "req"), None),
        P(("grp", "req"), None),
        P(("grp", "req")),
    )
    out_specs = (P(("grp", "req"), None), P(("grp", "req"), None))
    return jax.shard_map(body, mesh=mesh, in_specs=in_specs, out_specs=out_specs, check_vma=False)
```
